32 devices in a mesh: shard: 8 (over z, core), batch: 4 (over y, x).
Axes of the slice: x: 2, y: 2, z: 4, core: 2. Of those that a mesh axis runs over, the one named last changes fastest.
Arguments:
- data_inputs: bfloat16 [8, 256, 1024], P('shard', 'batch'), may hold values from -6 to 6
- data_targets: bfloat16 [8, 256, 512], P('shard', 'batch'), may hold values from -6 to 6
- row_picks: int32 [2, 8, 512], P(None, 'shard', 'batch'), may hold values from 0 to 63
- layer_one: float32 [8, 1024, 2048], P('shard', None, 'batch'), may hold values from -6 to 6
- layer_two: float32 [8, 2048, 512], P('shard', 'batch'), may hold values from -6 to 6
- noise_one: bfloat16 [2, 8, 1024, 2048], P(None, 'shard', None, 'batch'), may hold values from -6 to 6
- noise_two: bfloat16 [2, 8, 2048, 512], P(None, 'shard', 'batch'), may hold values from -6 to 6
Outputs:
- moved_one: float32 [8, 1024, 2048], P('shard', None, 'batch')
- moved_two: float32 [8, 2048, 512], P('shard', 'batch')
- last_errors: bfloat16 [8, 512, 512], P('shard', 'batch')
The draws below stay inside these ranges and needn't reach their ends.
All inputs are finite; a program needn't handle non-finite values.
Results may differ from the reference program's by a relative error of at most 0.014.
Values may be sent and summed in bfloat16 or wider, within the bound.
A program may use at most 64 MiB of HBM per device.

```python
import jax
import jax.numpy as jnp
from jax import lax

D_IN = 1024
HID = 2048
D_OUT = 512
ROWS_DEV = 128
DATA_DEV = 64
STEPS = 2
MB = 512
DATA = 256
CHAINS = 8
N_BATCH = 4


def with_ends(entries, rng, smallest, high):
    spot = [jax.random.randint(jax.random.fold_in(rng, axis), (), 0, length) for axis, length in enumerate(entries.shape)]
    main_axis = entries.shape.index(max(entries.shape))
    beside = spot[:main_axis] + [(spot[main_axis] + 1) % entries.shape[main_axis]] + spot[main_axis + 1:]
    return entries.at[tuple(spot)].set(smallest).at[tuple(beside)].set(high)


def block_levels(rng, shape, cuts, low, top_value):
    factor_of = 1.0
    for dim, parts in cuts:
        heights = jax.random.uniform(jax.random.fold_in(jax.random.fold_in(rng, 6), dim), (parts,), jnp.float32, low / len(cuts), top_value / len(cuts))
        factor_of = factor_of * jnp.repeat(jnp.exp(heights), shape[dim] // parts).reshape((-1,) + (1,) * (len(shape) - 1 - dim))
    return factor_of


def noise(key, dims, width, bound, pieces=(), held_as=jnp.bfloat16):
    level = block_levels(key, dims, pieces, -0.22, 0.18) if pieces else 1.0
    result = jax.random.normal(key, dims, jnp.float32) * width * level
    return jnp.minimum(jnp.maximum(result, -bound), bound).astype(held_as)


def setup_inputs(seed: int = 0) -> dict:
    splits = jax.random.split(jax.random.key(seed), 8)
    return {
        "data_inputs": noise(splits[0], (CHAINS, DATA, D_IN), 1.0, 6.0, ((0, 8), (1, 4))),
        "data_targets": noise(splits[1], (CHAINS, DATA, D_OUT), 1.0, 6.0, ((0, 8), (1, 4))),
        "row_picks": with_ends(jax.random.randint(splits[2], (STEPS, CHAINS, MB), 0, DATA_DEV), jax.random.fold_in(splits[2], 1), 0, DATA_DEV - 1).astype(jnp.int32),
        "layer_one": noise(splits[3], (CHAINS, D_IN, HID), 1.0, 6.0, ((0, 8), (2, 4)), jnp.float32),
        "layer_two": noise(splits[4], (CHAINS, HID, D_OUT), 1.0, 6.0, ((0, 8), (1, 4)), jnp.float32),
        "noise_one": noise(splits[5], (STEPS, CHAINS, D_IN, HID), 1.0, 6.0, ((1, 8), (3, 4))),
        "noise_two": noise(splits[6], (STEPS, CHAINS, HID, D_OUT), 1.0, 6.0, ((1, 8), (2, 4))),
    }


half_step = 0.01
root_step = 0.02 ** 0.5
precision_obs = 32.0


def one_chain(packed):
    data_x, data_y, picks, weights_a, weights_b, noise_a, noise_b = packed
    scale_in = D_IN ** -0.5
    scale_hid = HID ** -0.5
    group_width = HID // N_BATCH
    offsets = ((jnp.arange(MB) // ROWS_DEV) * DATA_DEV).astype(jnp.int32)
    last_out = jnp.zeros((MB, D_OUT), jnp.float32)
    for iteration in range(STEPS):
        chosen = picks[iteration].astype(jnp.int32) + offsets
        chosen_rows = data_x[chosen]
        chosen_targets = data_y[chosen].astype(jnp.float32)
        bf_a = weights_a.astype(jnp.bfloat16)
        bf_b = weights_b.astype(jnp.bfloat16)
        hidden = jnp.tanh(jnp.dot(chosen_rows, bf_a, preferred_element_type=jnp.float32) * scale_in)
        hidden_b = hidden.astype(jnp.bfloat16)
        grouped_h = hidden_b.reshape(MB, N_BATCH, group_width).astype(jnp.float32)
        grouped_w = bf_b.reshape(N_BATCH, group_width, D_OUT).astype(jnp.float32)
        shares = (jnp.einsum('mgk,gko->gmo', grouped_h, grouped_w) * scale_hid).astype(jnp.bfloat16)
        predicted = jnp.sum(shares.astype(jnp.float32), axis=0)
        errors_all = predicted - chosen_targets
        signal = (precision_obs * errors_all).astype(jnp.bfloat16)
        grad_two = jnp.dot(hidden_b.T, signal, preferred_element_type=jnp.float32) * scale_hid
        back_hidden = (jnp.dot(signal, bf_b.T, preferred_element_type=jnp.float32) * scale_hid
                       * (1.0 - hidden * hidden)).astype(jnp.bfloat16)
        grad_one = jnp.dot(chosen_rows.T, back_hidden, preferred_element_type=jnp.float32) * scale_in
        weights_a = weights_a - half_step * (grad_one + weights_a) + root_step * noise_a[iteration].astype(jnp.float32)
        weights_b = weights_b - half_step * (grad_two + weights_b) + root_step * noise_b[iteration].astype(jnp.float32)
        last_out = errors_all
    return weights_a, weights_b, last_out.astype(jnp.bfloat16)


def reference(data_inputs, data_targets, row_picks, layer_one, layer_two, noise_one, noise_two):
    packed = (data_inputs, data_targets, jnp.moveaxis(row_picks, 1, 0), layer_one, layer_two,
              jnp.moveaxis(noise_one, 1, 0), jnp.moveaxis(noise_two, 1, 0))
    final_a, final_b, last_errors = lax.map(one_chain, packed)
    return jnp.roll(final_a, 1, axis=0), jnp.roll(final_b, 1, axis=0), last_errors
```

```python
import functools

import jax
import jax.numpy as jnp
from jax import lax
from jax.experimental import pallas as pl
from jax.experimental.pallas import tpu as pltpu
from jax.sharding import PartitionSpec as P

D_IN = 1024
HID = 2048
STEPS = 2
half_step = 0.01
keep = 1.0 - half_step
root_step = 0.02**0.5
precision_obs = 32.0
scale_in = D_IN ** (-0.5)
scale_hid = HID ** (-0.5)
MESH = pl.DeviceIdType.MESH
TN = (((0,), (0,)), ((), ()))
NT = (((1,), (1,)), ((), ()))
f32 = jnp.float32
bf16 = jnp.bfloat16


def kernel(
    ns, nb, x_in, t_in, picks, l1, l2, n1h, n2h,
    d_out, x_out, c_out, m2_out, errs,
    x, w1, w2, n1, n2, w1b, w2b, h, hb, bh0, dsend, csend, m2send, share, share_in, sw,
    load_sem, xs_sem, xr_sem, ss_sem, sr_sem, gs_sem, gr_sem, hs_sem, hr_sem,
):
    s = lax.axis_index("shard")
    b = lax.axis_index("batch")
    nxt = (lax.rem(s + 1, ns), b)
    prv = (lax.rem(s + ns - 1, ns), b)
    rows = x_in.shape[0]

    loads = [
        pltpu.make_async_copy(src, dst, load_sem.at[i])
        for i, (src, dst) in enumerate(((l1, w1), (n1h, n1), (l2, w2), (n2h, n2)))
    ]
    for load in loads:
        load.start()

    barrier = pltpu.get_barrier_semaphore()
    peers = [(s, lax.rem(b + k, nb)) for k in range(nb)]
    owners = [(s, lax.rem(b + nb - k, nb)) for k in range(nb)]
    for who in peers[1:] + [nxt, prv]:
        pl.semaphore_signal(barrier, inc=1, device_id=who, device_id_type=MESH)
    pl.semaphore_wait(barrier, nb + 1)

    sends = []

    def remote(src, dst, send, recv, who):
        copy = pltpu.make_async_remote_copy(
            src_ref=src, dst_ref=dst, send_sem=send, recv_sem=recv,
            device_id=who, device_id_type=MESH,
        )
        copy.start()
        sends.append(copy)
        return copy

    def slot(k):
        return pl.ds(k * rows, rows)

    gathers = [
        remote(x_in, x.at[slot(k)], xs_sem.at[k], xr_sem.at[k], peers[k])
        for k in range(1, nb)
    ]
    x[slot(0), :] = x_in[...]

    loads[0].wait()
    loads[1].wait()
    hops = []
    quarter = D_IN // 4
    for q in range(4):
        @pl.loop(0, quarter, step=32)
        def _(r, q=q):
            part = pl.ds(q * quarter + r, 32)
            w = w1[part, :]
            w1b[part, :] = w.astype(bf16)
            w = keep * w + root_step * n1[0, part, :].astype(f32)
            w1[part, :] = w
            dsend[part, :] = (keep * w + root_step * n1[1, part, :].astype(f32)).astype(bf16)
        piece = pl.ds(q * quarter, quarter)
        hops.append(remote(dsend.at[piece], d_out.at[piece], hs_sem.at[q], hr_sem.at[q], nxt))
    loads[2].wait()
    loads[3].wait()
    for copy in gathers:
        copy.wait_recv()
    hops.append(remote(x, x_out, hs_sem.at[4], hr_sem.at[4], nxt))

    for step in range(STEPS):
        w2b[...] = w2[...].astype(bf16)
        hidden = jnp.tanh(jnp.dot(x[...], w1b[...], preferred_element_type=f32) * scale_in)
        h[...] = hidden
        hb[...] = hidden.astype(bf16)
        share[step] = (
            jnp.dot(hb[...], w2b[...], preferred_element_type=f32) * scale_hid
        ).astype(bf16)
        scatters = [
            remote(
                share.at[step, slot(k)], share_in.at[step, k],
                ss_sem.at[step, k], sr_sem.at[step, k], owners[k],
            )
            for k in range(1, nb)
        ]
        @pl.loop(0, w2.shape[0], step=32)
        def _(r):
            part = pl.ds(r, 32)
            w2[part, :] = keep * w2[part, :] + root_step * n2[step, part, :].astype(f32)

        picked = lax.broadcasted_iota(jnp.int32, (rows, picks.shape[2]), 0) == picks[step]
        picked = jnp.where(picked, 1.0, 0.0)
        counts = jnp.sum(picked, axis=1, keepdims=True)
        predicted = share[step, slot(0), :].astype(f32)
        for k in range(1, nb):
            scatters[k - 1].wait_recv()
            predicted = predicted + share_in[step, k].astype(f32)
        errors = predicted - t_in[...].astype(f32)
        signal = (precision_obs * errors).astype(bf16).astype(f32)
        sw[step, slot(0), :] = (counts * signal).astype(bf16)
        signals = [
            remote(
                sw.at[step, slot(0)], sw.at[step, slot(k)],
                gs_sem.at[step, k], gr_sem.at[step, k], peers[k],
            )
            for k in range(1, nb)
        ]
        if step == STEPS - 1:
            errs[...] = lax.dot_general(
                picked.astype(bf16), errors.astype(bf16), TN, preferred_element_type=f32
            ).astype(bf16)
        for copy in signals:
            copy.wait_recv()
        back = (
            lax.dot_general(sw[step], w2b[...], NT, preferred_element_type=f32)
            * scale_hid
            * (1.0 - h[...] * h[...])
        )
        if step == 0:
            bh0[...] = back.astype(bf16)
        else:
            csend[...] = (keep * bh0[...].astype(f32) + back).astype(bf16)
            hops.append(remote(csend, c_out, hs_sem.at[5], hr_sem.at[5], nxt))
        grad_two = lax.dot_general(hb[...], sw[step], TN, preferred_element_type=f32)
        final_two = w2[...] - (half_step * scale_hid) * grad_two
        if step == 0:
            w2[...] = final_two
            for q in range(4):
                piece = pl.ds(q * quarter, quarter)
                grad_one = lax.dot_general(x[:, piece], bh0[...], TN, preferred_element_type=f32)
                w1b[piece, :] = (w1[piece, :] - (half_step * scale_in) * grad_one).astype(bf16)
        else:
            m2send[...] = final_two.astype(bf16)
            hops.append(remote(m2send, m2_out, hs_sem.at[6], hr_sem.at[6], nxt))
    for copy in hops:
        copy.wait_recv()
    for copy in sends:
        copy.wait_send()


def per_device(ns, nb, data_inputs, data_targets, row_picks, layer_one, layer_two, noise_one, noise_two):
    x_in, t_in, l1, l2 = data_inputs[0], data_targets[0], layer_one[0], layer_two[0]
    n1h, n2h = noise_one[:, 0], noise_two[:, 0]
    rows, d_in = x_in.shape
    d_out = t_in.shape[1]
    hid = l1.shape[1]
    total = rows * nb
    mine = row_picks.shape[2]
    any_spec = pl.BlockSpec(memory_space=pl.ANY)
    vmem = pl.BlockSpec(memory_space=pltpu.VMEM)
    V = pltpu.VMEM
    D = pltpu.SemaphoreType.DMA
    dd, xx, cc, m2, errs = pl.pallas_call(
        functools.partial(kernel, ns, nb),
        out_shape=(
            jax.ShapeDtypeStruct((d_in, hid), bf16),
            jax.ShapeDtypeStruct((total, d_in), bf16),
            jax.ShapeDtypeStruct((total, hid), bf16),
            jax.ShapeDtypeStruct((hid, d_out), bf16),
            jax.ShapeDtypeStruct((mine, d_out), bf16),
        ),
        in_specs=[vmem] * 3 + [any_spec] * 4,
        out_specs=(any_spec,) * 4 + (vmem,),
        scratch_shapes=[
            V((total, d_in), bf16),
            V((d_in, hid), f32),
            V((hid, d_out), f32),
            V((STEPS, d_in, hid), bf16),
            V((STEPS, hid, d_out), bf16),
            V((d_in, hid), bf16),
            V((hid, d_out), bf16),
            V((total, hid), f32),
            V((total, hid), bf16),
            V((total, hid), bf16),
            V((d_in, hid), bf16),
            V((total, hid), bf16),
            V((hid, d_out), bf16),
            V((STEPS, total, d_out), bf16),
            V((STEPS, nb, rows, d_out), bf16),
            V((STEPS, total, d_out), bf16),
            D((4,)), D((nb,)), D((nb,)),
            D((STEPS, nb)), D((STEPS, nb)), D((STEPS, nb)), D((STEPS, nb)),
            D((7,)), D((7,)),
        ],
        compiler_params=pltpu.CompilerParams(
            collective_id=0, has_side_effects=True, vmem_limit_bytes=40 * 1024 * 1024
        ),
    )(x_in, t_in, row_picks, l1, l2, n1h, n2h)
    grad = lax.dot_general(xx, cc, TN, preferred_element_type=f32)
    moved_a = dd.astype(f32) - (half_step * scale_in) * grad
    return moved_a[None], m2.astype(f32)[None], errs[None]


def solution(mesh):
    in_specs = (
        P("shard", "batch", None),
        P("shard", "batch", None),
        P(None, "shard", "batch"),
        P("shard", None, "batch"),
        P("shard", "batch", None),
        P(None, "shard", None, "batch"),
        P(None, "shard", "batch", None),
    )
    out_specs = (P("shard", None, "batch"), P("shard", "batch", None), P("shard", "batch", None))
    return jax.shard_map(
        functools.partial(per_device, mesh.shape["shard"], mesh.shape["batch"]),
        mesh=mesh, in_specs=in_specs, out_specs=out_specs, check_vma=False,
    )
```

```python
import functools

import jax
import jax.numpy as jnp
from jax import lax
from jax.experimental import pallas as pl
from jax.experimental.pallas import tpu as pltpu
from jax.sharding import PartitionSpec as P

D_IN = 1024
HID = 2048
STEPS = 2
half_step = 0.01
keep = 1.0 - half_step
root_step = 0.02**0.5
precision_obs = 32.0
scale_in = D_IN ** (-0.5)
scale_hid = HID ** (-0.5)
MESH = pl.DeviceIdType.MESH
TN = (((0,), (0,)), ((), ()))
NT = (((1,), (1,)), ((), ()))
f32 = jnp.float32
bf16 = jnp.bfloat16


def kernel(
    ns, nb, x_in, t_in, picks, l1, l2, n1h, n2h,
    d_out, x_out, c_out, m2_out, errs,
    x, w1, w2, n1, n2, w1b, w2b, h, hb, bh0, dsend, csend, m2send, share, share_in, sw,
    load_sem, xs_sem, xr_sem, ss_sem, sr_sem, gs_sem, gr_sem, hs_sem, hr_sem, fs_sem, fr_sem,
):
    s = lax.axis_index("shard")
    b = lax.axis_index("batch")
    nxt = (lax.rem(s + 1, ns), b)
    prv = (lax.rem(s + ns - 1, ns), b)
    rows = x_in.shape[0]

    loads = [
        pltpu.make_async_copy(src, dst, load_sem.at[i])
        for i, (src, dst) in enumerate(((l1, w1), (n1h, n1), (l2, w2), (n2h, n2)))
    ]
    for load in loads:
        load.start()

    barrier = pltpu.get_barrier_semaphore()
    peers = [(s, lax.rem(b + k, nb)) for k in range(nb)]
    owners = [(s, lax.rem(b + nb - k, nb)) for k in range(nb)]
    for who in peers[1:] + [nxt, prv]:
        pl.semaphore_signal(barrier, inc=1, device_id=who, device_id_type=MESH)
    pl.semaphore_wait(barrier, nb + 1)

    sends = []

    def remote(src, dst, send, recv, who):
        copy = pltpu.make_async_remote_copy(
            src_ref=src, dst_ref=dst, send_sem=send, recv_sem=recv,
            device_id=who, device_id_type=MESH,
        )
        copy.start()
        sends.append(copy)
        return copy

    def slot(k):
        return pl.ds(k * rows, rows)

    gathers = [
        remote(x_in, x.at[slot(k)], xs_sem.at[k], xr_sem.at[k], peers[k])
        for k in range(1, nb)
    ]
    passed = remote(x_in, x_out.at[slot(0)], hs_sem.at[4], hr_sem.at[4], nxt)
    x[slot(0), :] = x_in[...]

    loads[0].wait()
    loads[1].wait()
    hops = []
    quarter = D_IN // 4
    for q in range(4):
        @pl.loop(0, quarter, step=32)
        def _(r, q=q):
            part = pl.ds(q * quarter + r, 32)
            w = w1[part, :]
            w1b[part, :] = w.astype(bf16)
            w = keep * w + root_step * n1[0, part, :].astype(f32)
            w1[part, :] = w
            dsend[part, :] = (keep * w + root_step * n1[1, part, :].astype(f32)).astype(bf16)
        piece = pl.ds(q * quarter, quarter)
        hops.append(remote(dsend.at[piece], d_out.at[piece], hs_sem.at[q], hr_sem.at[q], nxt))
    loads[2].wait()
    loads[3].wait()
    for copy in gathers:
        copy.wait_recv()

    for step in range(STEPS):
        w2b[...] = w2[...].astype(bf16)
        hidden = jnp.tanh(jnp.dot(x[...], w1b[...], preferred_element_type=f32) * scale_in)
        h[...] = hidden
        hb[...] = hidden.astype(bf16)
        share[step] = (
            jnp.dot(hb[...], w2b[...], preferred_element_type=f32) * scale_hid
        ).astype(bf16)
        scatters = [
            remote(
                share.at[step, slot(k)], share_in.at[step, k],
                ss_sem.at[step, k], sr_sem.at[step, k], owners[k],
            )
            for k in range(1, nb)
        ]
        if step == 0:
            passed.wait_recv()
            hops += [
                remote(x_out.at[slot(0)], x_out.at[slot(k)], fs_sem.at[k], fr_sem.at[k], peers[k])
                for k in range(1, nb)
            ]

        @pl.loop(0, w2.shape[0], step=32)
        def _(r):
            part = pl.ds(r, 32)
            w2[part, :] = keep * w2[part, :] + root_step * n2[step, part, :].astype(f32)

        picked = lax.broadcasted_iota(jnp.int32, (rows, picks.shape[2]), 0) == picks[step]
        picked = jnp.where(picked, 1.0, 0.0)
        counts = jnp.sum(picked, axis=1, keepdims=True)
        predicted = share[step, slot(0), :].astype(f32)
        for k in range(1, nb):
            scatters[k - 1].wait_recv()
            predicted = predicted + share_in[step, k].astype(f32)
        errors = predicted - t_in[...].astype(f32)
        signal = (precision_obs * errors).astype(bf16).astype(f32)
        sw[step, slot(0), :] = (counts * signal).astype(bf16)
        signals = [
            remote(
                sw.at[step, slot(0)], sw.at[step, slot(k)],
                gs_sem.at[step, k], gr_sem.at[step, k], peers[k],
            )
            for k in range(1, nb)
        ]
        if step == STEPS - 1:
            errs[...] = lax.dot_general(
                picked.astype(bf16), errors.astype(bf16), TN, preferred_element_type=f32
            ).astype(bf16)
        for copy in signals:
            copy.wait_recv()
        back = (
            lax.dot_general(sw[step], w2b[...], NT, preferred_element_type=f32)
            * scale_hid
            * (1.0 - h[...] * h[...])
        )
        if step == 0:
            bh0[...] = back.astype(bf16)
        else:
            csend[...] = (keep * bh0[...].astype(f32) + back).astype(bf16)
            hops.append(remote(csend, c_out, hs_sem.at[5], hr_sem.at[5], nxt))
        grad_two = lax.dot_general(hb[...], sw[step], TN, preferred_element_type=f32)
        final_two = w2[...] - (half_step * scale_hid) * grad_two
        if step == 0:
            w2[...] = final_two
            for q in range(4):
                piece = pl.ds(q * quarter, quarter)
                grad_one = lax.dot_general(x[:, piece], bh0[...], TN, preferred_element_type=f32)
                w1b[piece, :] = (w1[piece, :] - (half_step * scale_in) * grad_one).astype(bf16)
        else:
            m2send[...] = final_two.astype(bf16)
            hops.append(remote(m2send, m2_out, hs_sem.at[6], hr_sem.at[6], nxt))
    for copy in hops:
        copy.wait_recv()
    for copy in sends:
        copy.wait_send()


def per_device(ns, nb, data_inputs, data_targets, row_picks, layer_one, layer_two, noise_one, noise_two):
    x_in, t_in, l1, l2 = data_inputs[0], data_targets[0], layer_one[0], layer_two[0]
    n1h, n2h = noise_one[:, 0], noise_two[:, 0]
    rows, d_in = x_in.shape
    d_out = t_in.shape[1]
    hid = l1.shape[1]
    total = rows * nb
    mine = row_picks.shape[2]
    any_spec = pl.BlockSpec(memory_space=pl.ANY)
    vmem = pl.BlockSpec(memory_space=pltpu.VMEM)
    V = pltpu.VMEM
    D = pltpu.SemaphoreType.DMA
    dd, xx, cc, m2, errs = pl.pallas_call(
        functools.partial(kernel, ns, nb),
        out_shape=(
            jax.ShapeDtypeStruct((d_in, hid), bf16),
            jax.ShapeDtypeStruct((total, d_in), bf16),
            jax.ShapeDtypeStruct((total, hid), bf16),
            jax.ShapeDtypeStruct((hid, d_out), bf16),
            jax.ShapeDtypeStruct((mine, d_out), bf16),
        ),
        in_specs=[vmem] * 3 + [any_spec] * 4,
        out_specs=(any_spec,) * 4 + (vmem,),
        scratch_shapes=[
            V((total, d_in), bf16),
            V((d_in, hid), f32),
            V((hid, d_out), f32),
            V((STEPS, d_in, hid), bf16),
            V((STEPS, hid, d_out), bf16),
            V((d_in, hid), bf16),
            V((hid, d_out), bf16),
            V((total, hid), f32),
            V((total, hid), bf16),
            V((total, hid), bf16),
            V((d_in, hid), bf16),
            V((total, hid), bf16),
            V((hid, d_out), bf16),
            V((STEPS, total, d_out), bf16),
            V((STEPS, nb, rows, d_out), bf16),
            V((STEPS, total, d_out), bf16),
            D((4,)), D((nb,)), D((nb,)),
            D((STEPS, nb)), D((STEPS, nb)), D((STEPS, nb)), D((STEPS, nb)),
            D((7,)), D((7,)), D((nb,)), D((nb,)),
        ],
        compiler_params=pltpu.CompilerParams(
            collective_id=0, has_side_effects=True, vmem_limit_bytes=60 * 1024 * 1024
        ),
    )(x_in, t_in, row_picks, l1, l2, n1h, n2h)
    grad = lax.dot_general(xx, cc, TN, preferred_element_type=f32)
    moved_a = dd.astype(f32) - (half_step * scale_in) * grad
    return moved_a[None], m2.astype(f32)[None], errs[None]


def solution(mesh):
    in_specs = (
        P("shard", "batch", None),
        P("shard", "batch", None),
        P(None, "shard", "batch"),
        P("shard", None, "batch"),
        P("shard", "batch", None),
        P(None, "shard", None, "batch"),
        P(None, "shard", "batch", None),
    )
    out_specs = (P("shard", None, "batch"), P("shard", "batch", None), P("shard", "batch", None))
    return jax.shard_map(
        functools.partial(per_device, mesh.shape["shard"], mesh.shape["batch"]),
        mesh=mesh, in_specs=in_specs, out_specs=out_specs, check_vma=False,
    )
```

```python
import functools

import jax
import jax.numpy as jnp
from jax import lax
from jax.experimental import pallas as pl
from jax.experimental.pallas import tpu as pltpu
from jax.sharding import PartitionSpec as P

D_IN = 1024
HID = 2048
STEPS = 2
half_step = 0.01
keep = 1.0 - half_step
root_step = 0.02**0.5
precision_obs = 32.0
scale_in = D_IN ** (-0.5)
scale_hid = HID ** (-0.5)
MESH = pl.DeviceIdType.MESH
TN = (((0,), (0,)), ((), ()))
NT = (((1,), (1,)), ((), ()))
f32 = jnp.float32
bf16 = jnp.bfloat16


def kernel(
    ns, nb, x_in, t_in, picks, l1, l2, n1h, n2h,
    d_out, x_out, c_out, m2_out, errs,
    x, w1, w2, n1, n2, w1b, w2b, h, hb, bh0, dsend, csend, m2send, share, share_in, sw,
    load_sem, xs_sem, xr_sem, ss_sem, sr_sem, gs_sem, gr_sem, hs_sem, hr_sem, fs_sem, fr_sem,
):
    s = lax.axis_index("shard")
    b = lax.axis_index("batch")
    nxt = (lax.rem(s + 1, ns), b)
    prv = (lax.rem(s + ns - 1, ns), b)
    rows = x_in.shape[0]

    quarter = D_IN // 4
    pairs = []
    for q in range(4):
        piece = pl.ds(q * quarter, quarter)
        pairs += [(l1.at[piece], w1.at[piece])]
        pairs += [(n1h.at[i, piece], n1.at[i, piece]) for i in range(STEPS)]
    pairs += [(l2, w2)] + [(n2h.at[i], n2.at[i]) for i in range(STEPS)]
    loads = [
        pltpu.make_async_copy(src, dst, load_sem.at[i]) for i, (src, dst) in enumerate(pairs)
    ]
    for load in loads:
        load.start()

    barrier = pltpu.get_barrier_semaphore()
    peers = [(s, lax.rem(b + k, nb)) for k in range(nb)]
    owners = [(s, lax.rem(b + nb - k, nb)) for k in range(nb)]
    for who in peers[1:] + [nxt, prv]:
        pl.semaphore_signal(barrier, inc=1, device_id=who, device_id_type=MESH)
    pl.semaphore_wait(barrier, nb + 1)

    sends = []

    def remote(src, dst, send, recv, who):
        copy = pltpu.make_async_remote_copy(
            src_ref=src, dst_ref=dst, send_sem=send, recv_sem=recv,
            device_id=who, device_id_type=MESH,
        )
        copy.start()
        sends.append(copy)
        return copy

    def slot(k):
        return pl.ds(k * rows, rows)

    gathers = [
        remote(x_in, x.at[slot(k)], xs_sem.at[k], xr_sem.at[k], peers[k])
        for k in range(1, nb)
    ]
    passed = remote(x_in, x_out.at[slot(0)], hs_sem.at[4], hr_sem.at[4], nxt)
    x[slot(0), :] = x_in[...]

    hops = []
    for q in range(4):
        for load in loads[3 * q : 3 * q + 3]:
            load.wait()

        @pl.loop(0, quarter, step=32)
        def _(r, q=q):
            part = pl.ds(q * quarter + r, 32)
            w = w1[part, :]
            w1b[part, :] = w.astype(bf16)
            w = keep * w + root_step * n1[0, part, :].astype(f32)
            w1[part, :] = w
            dsend[part, :] = (keep * w + root_step * n1[1, part, :].astype(f32)).astype(bf16)
        piece = pl.ds(q * quarter, quarter)
        hops.append(remote(dsend.at[piece], d_out.at[piece], hs_sem.at[q], hr_sem.at[q], nxt))
    for load in loads[12:]:
        load.wait()
    for copy in gathers:
        copy.wait_recv()

    for step in range(STEPS):
        w2b[...] = w2[...].astype(bf16)
        hidden = jnp.tanh(jnp.dot(x[...], w1b[...], preferred_element_type=f32) * scale_in)
        h[...] = hidden
        hb[...] = hidden.astype(bf16)
        share[step] = (
            jnp.dot(hb[...], w2b[...], preferred_element_type=f32) * scale_hid
        ).astype(bf16)
        scatters = [
            remote(
                share.at[step, slot(k)], share_in.at[step, k],
                ss_sem.at[step, k], sr_sem.at[step, k], owners[k],
            )
            for k in range(1, nb)
        ]
        if step == 0:
            passed.wait_recv()
            hops += [
                remote(x_out.at[slot(0)], x_out.at[slot(k)], fs_sem.at[k], fr_sem.at[k], peers[k])
                for k in range(1, nb)
            ]

        @pl.loop(0, w2.shape[0], step=32)
        def _(r):
            part = pl.ds(r, 32)
            w2[part, :] = keep * w2[part, :] + root_step * n2[step, part, :].astype(f32)

        picked = lax.broadcasted_iota(jnp.int32, (rows, picks.shape[2]), 0) == picks[step]
        picked = jnp.where(picked, 1.0, 0.0)
        counts = jnp.sum(picked, axis=1, keepdims=True)
        predicted = share[step, slot(0), :].astype(f32)
        for k in range(1, nb):
            scatters[k - 1].wait_recv()
            predicted = predicted + share_in[step, k].astype(f32)
        errors = predicted - t_in[...].astype(f32)
        signal = (precision_obs * errors).astype(bf16).astype(f32)
        sw[step, slot(0), :] = (counts * signal).astype(bf16)
        signals = [
            remote(
                sw.at[step, slot(0)], sw.at[step, slot(k)],
                gs_sem.at[step, k], gr_sem.at[step, k], peers[k],
            )
            for k in range(1, nb)
        ]
        if step == STEPS - 1:
            errs[...] = lax.dot_general(
                picked.astype(bf16), errors.astype(bf16), TN, preferred_element_type=f32
            ).astype(bf16)
        for copy in signals:
            copy.wait_recv()
        back = (
            lax.dot_general(sw[step], w2b[...], NT, preferred_element_type=f32)
            * scale_hid
            * (1.0 - h[...] * h[...])
        )
        if step == 0:
            bh0[...] = back.astype(bf16)
        else:
            csend[...] = (keep * bh0[...].astype(f32) + back).astype(bf16)
            hops.append(remote(csend, c_out, hs_sem.at[5], hr_sem.at[5], nxt))
        grad_two = lax.dot_general(hb[...], sw[step], TN, preferred_element_type=f32)
        final_two = w2[...] - (half_step * scale_hid) * grad_two
        if step == 0:
            w2[...] = final_two
            for q in range(4):
                piece = pl.ds(q * quarter, quarter)
                grad_one = lax.dot_general(x[:, piece], bh0[...], TN, preferred_element_type=f32)
                w1b[piece, :] = (w1[piece, :] - (half_step * scale_in) * grad_one).astype(bf16)
        else:
            m2send[...] = final_two.astype(bf16)
            hops.append(remote(m2send, m2_out, hs_sem.at[6], hr_sem.at[6], nxt))
    for copy in hops:
        copy.wait_recv()
    for copy in sends:
        copy.wait_send()


def per_device(ns, nb, data_inputs, data_targets, row_picks, layer_one, layer_two, noise_one, noise_two):
    x_in, t_in, l1, l2 = data_inputs[0], data_targets[0], layer_one[0], layer_two[0]
    n1h, n2h = noise_one[:, 0], noise_two[:, 0]
    rows, d_in = x_in.shape
    d_out = t_in.shape[1]
    hid = l1.shape[1]
    total = rows * nb
    mine = row_picks.shape[2]
    any_spec = pl.BlockSpec(memory_space=pl.ANY)
    vmem = pl.BlockSpec(memory_space=pltpu.VMEM)
    V = pltpu.VMEM
    D = pltpu.SemaphoreType.DMA
    dd, xx, cc, m2, errs = pl.pallas_call(
        functools.partial(kernel, ns, nb),
        out_shape=(
            jax.ShapeDtypeStruct((d_in, hid), bf16),
            jax.ShapeDtypeStruct((total, d_in), bf16),
            jax.ShapeDtypeStruct((total, hid), bf16),
            jax.ShapeDtypeStruct((hid, d_out), bf16),
            jax.ShapeDtypeStruct((mine, d_out), bf16),
        ),
        in_specs=[vmem] * 3 + [any_spec] * 4,
        out_specs=(any_spec,) * 4 + (vmem,),
        scratch_shapes=[
            V((total, d_in), bf16),
            V((d_in, hid), f32),
            V((hid, d_out), f32),
            V((STEPS, d_in, hid), bf16),
            V((STEPS, hid, d_out), bf16),
            V((d_in, hid), bf16),
            V((hid, d_out), bf16),
            V((total, hid), f32),
            V((total, hid), bf16),
            V((total, hid), bf16),
            V((d_in, hid), bf16),
            V((total, hid), bf16),
            V((hid, d_out), bf16),
            V((STEPS, total, d_out), bf16),
            V((STEPS, nb, rows, d_out), bf16),
            V((STEPS, total, d_out), bf16),
            D((15,)), D((nb,)), D((nb,)),
            D((STEPS, nb)), D((STEPS, nb)), D((STEPS, nb)), D((STEPS, nb)),
            D((7,)), D((7,)), D((nb,)), D((nb,)),
        ],
        compiler_params=pltpu.CompilerParams(
            collective_id=0, has_side_effects=True, vmem_limit_bytes=60 * 1024 * 1024
        ),
    )(x_in, t_in, row_picks, l1, l2, n1h, n2h)
    grad = lax.dot_general(xx, cc, TN, preferred_element_type=f32)
    moved_a = dd.astype(f32) - (half_step * scale_in) * grad
    return moved_a[None], m2.astype(f32)[None], errs[None]


def solution(mesh):
    in_specs = (
        P("shard", "batch", None),
        P("shard", "batch", None),
        P(None, "shard", "batch"),
        P("shard", None, "batch"),
        P("shard", "batch", None),
        P(None, "shard", None, "batch"),
        P(None, "shard", "batch", None),
    )
    out_specs = (P("shard", None, "batch"), P("shard", "batch", None), P("shard", "batch", None))
    return jax.shard_map(
        functools.partial(per_device, mesh.shape["shard"], mesh.shape["batch"]),
        mesh=mesh, in_specs=in_specs, out_specs=out_specs, check_vma=False,
    )
```

```python
import functools

import jax
import jax.numpy as jnp
from jax import lax
from jax.experimental import pallas as pl
from jax.experimental.pallas import tpu as pltpu
from jax.sharding import PartitionSpec as P

D_IN = 1024
HID = 2048
STEPS = 2
half_step = 0.01
keep = 1.0 - half_step
root_step = 0.02**0.5
precision_obs = 32.0
scale_in = D_IN ** (-0.5)
scale_hid = HID ** (-0.5)
MESH = pl.DeviceIdType.MESH
TN = (((0,), (0,)), ((), ()))
NT = (((1,), (1,)), ((), ()))
f32 = jnp.float32
bf16 = jnp.bfloat16


def kernel(
    ns, nb, x_in, t_in, picks, l1, l2, n1h, n2h,
    d_out, x_out, c_out, m2_out, errs,
    x, w1, w2, n1, n2, w1b, w2b, h, hb, bh0, dsend, csend, m2send, share, share_in, sw,
    load_sem, xs_sem, xr_sem, ss_sem, sr_sem, gs_sem, gr_sem, hs_sem, hr_sem, fs_sem, fr_sem,
):
    s = lax.axis_index("shard")
    b = lax.axis_index("batch")
    nxt = (lax.rem(s + 1, ns), b)
    prv = (lax.rem(s + ns - 1, ns), b)
    rows = x_in.shape[0]

    quarter = D_IN // 4
    pairs = []
    for q in range(4):
        piece = pl.ds(q * quarter, quarter)
        pairs += [(l1.at[piece], w1.at[piece])]
        pairs += [(n1h.at[i, piece], n1.at[i, piece]) for i in range(STEPS)]
    pairs += [(l2, w2)] + [(n2h.at[i], n2.at[i]) for i in range(STEPS)]
    loads = [
        pltpu.make_async_copy(src, dst, load_sem.at[i]) for i, (src, dst) in enumerate(pairs)
    ]
    for load in loads:
        load.start()

    barrier = pltpu.get_barrier_semaphore()
    peers = [(s, lax.rem(b + k, nb)) for k in range(nb)]
    owners = [(s, lax.rem(b + nb - k, nb)) for k in range(nb)]
    for who in peers[1:] + [nxt, prv]:
        pl.semaphore_signal(barrier, inc=1, device_id=who, device_id_type=MESH)
    pl.semaphore_wait(barrier, nb + 1)

    sends = []

    def remote(src, dst, send, recv, who):
        copy = pltpu.make_async_remote_copy(
            src_ref=src, dst_ref=dst, send_sem=send, recv_sem=recv,
            device_id=who, device_id_type=MESH,
        )
        copy.start()
        sends.append(copy)
        return copy

    def slot(k):
        return pl.ds(k * rows, rows)

    gathers = [
        remote(x_in, x.at[slot(k)], xs_sem.at[k], xr_sem.at[k], peers[k])
        for k in range(1, nb)
    ]
    passed = remote(x_in, x_out.at[slot(0)], hs_sem.at[4], hr_sem.at[4], nxt)
    x[slot(0), :] = x_in[...]

    hops = []
    for q in range(4):
        for load in loads[3 * q : 3 * q + 3]:
            load.wait()

        @pl.loop(0, quarter, step=32)
        def _(r, q=q):
            part = pl.ds(q * quarter + r, 32)
            w = w1[part, :]
            w1b[part, :] = w.astype(bf16)
            w = keep * w + root_step * n1[0, part, :].astype(f32)
            w1[part, :] = w
            dsend[part, :] = (keep * w + root_step * n1[1, part, :].astype(f32)).astype(bf16)
        piece = pl.ds(q * quarter, quarter)
        hops.append(remote(dsend.at[piece], d_out.at[piece], hs_sem.at[q], hr_sem.at[q], nxt))
    for load in loads[12:]:
        load.wait()
    for copy in gathers:
        copy.wait_recv()

    for step in range(STEPS):
        w2b[...] = w2[...].astype(bf16)
        hidden = jnp.tanh(jnp.dot(x[...], w1b[...], preferred_element_type=f32) * scale_in)
        h[...] = hidden
        hb[...] = hidden.astype(bf16)
        share[step] = (
            jnp.dot(hb[...], w2b[...], preferred_element_type=f32) * scale_hid
        ).astype(bf16)
        scatters = [
            remote(
                share.at[step, slot(k)], share_in.at[step, k],
                ss_sem.at[step, k], sr_sem.at[step, k], owners[k],
            )
            for k in range(1, nb)
        ]
        if step == 0:
            passed.wait_recv()
            hops += [
                remote(x_out.at[slot(0)], x_out.at[slot(k)], fs_sem.at[k], fr_sem.at[k], peers[k])
                for k in range(1, nb)
            ]

        @pl.loop(0, w2.shape[0], step=32)
        def _(r):
            part = pl.ds(r, 32)
            w2[part, :] = keep * w2[part, :] + root_step * n2[step, part, :].astype(f32)

        picked = lax.broadcasted_iota(jnp.int32, (rows, picks.shape[2]), 0) == picks[step]
        picked = jnp.where(picked, 1.0, 0.0)
        counts = jnp.sum(picked, axis=1, keepdims=True)
        predicted = share[step, slot(0), :].astype(f32)
        for k in range(1, nb):
            scatters[k - 1].wait_recv()
            predicted = predicted + share_in[step, k].astype(f32)
        errors = predicted - t_in[...].astype(f32)
        signal = (precision_obs * errors).astype(bf16).astype(f32)
        sw[step, slot(0), :] = (counts * signal).astype(bf16)
        signals = [
            remote(
                sw.at[step, slot(0)], sw.at[step, slot(k)],
                gs_sem.at[step, k], gr_sem.at[step, k], peers[k],
            )
            for k in range(1, nb)
        ]
        if step == STEPS - 1:
            errs[...] = lax.dot_general(
                picked.astype(bf16), errors.astype(bf16), TN, preferred_element_type=f32
            ).astype(bf16)
        for copy in signals:
            copy.wait_recv()
        back = (
            lax.dot_general(sw[step], w2b[...], NT, preferred_element_type=f32)
            * scale_hid
            * (1.0 - h[...] * h[...])
        )
        if step == 0:
            bh0[...] = back.astype(bf16)
        else:
            csend[...] = (keep * bh0[...].astype(f32) + back).astype(bf16)
            hops.append(remote(csend, c_out, hs_sem.at[5], hr_sem.at[5], nxt))
        grad_two = lax.dot_general(hb[...], sw[step], TN, preferred_element_type=f32)
        final_two = w2[...] - (half_step * scale_hid) * grad_two
        if step == 0:
            w2[...] = final_two
            for q in range(4):
                piece = pl.ds(q * quarter, quarter)
                grad_one = lax.dot_general(x[:, piece], bh0[...], TN, preferred_element_type=f32)
                w1b[piece, :] = (w1[piece, :] - (half_step * scale_in) * grad_one).astype(bf16)
        else:
            m2send[...] = final_two.astype(bf16)
            hops.append(remote(m2send, m2_out, hs_sem.at[6], hr_sem.at[6], nxt))
    for copy in hops:
        copy.wait_recv()
    for copy in sends:
        copy.wait_send()


def per_device(ns, nb, data_inputs, data_targets, row_picks, layer_one, layer_two, noise_one, noise_two):
    x_in, t_in, l1, l2 = data_inputs[0], data_targets[0], layer_one[0], layer_two[0]
    n1h, n2h = noise_one[:, 0], noise_two[:, 0]
    rows, d_in = x_in.shape
    d_out = t_in.shape[1]
    hid = l1.shape[1]
    total = rows * nb
    mine = row_picks.shape[2]
    any_spec = pl.BlockSpec(memory_space=pl.ANY)
    vmem = pl.BlockSpec(memory_space=pltpu.VMEM)
    V = pltpu.VMEM
    D = pltpu.SemaphoreType.DMA
    dd, xx, cc, m2, errs = pl.pallas_call(
        functools.partial(kernel, ns, nb),
        out_shape=(
            jax.ShapeDtypeStruct((d_in, hid), bf16),
            jax.ShapeDtypeStruct((total, d_in), bf16),
            jax.ShapeDtypeStruct((total, hid), bf16),
            jax.ShapeDtypeStruct((hid, d_out), bf16),
            jax.ShapeDtypeStruct((mine, d_out), bf16),
        ),
        in_specs=[vmem] * 3 + [any_spec] * 4,
        out_specs=(any_spec,) * 4 + (vmem,),
        scratch_shapes=[
            V((total, d_in), bf16),
            V((d_in, hid), f32),
            V((hid, d_out), f32),
            V((STEPS, d_in, hid), bf16),
            V((STEPS, hid, d_out), bf16),
            V((d_in, hid), bf16),
            V((hid, d_out), bf16),
            V((total, hid), f32),
            V((total, hid), bf16),
            V((total, hid), bf16),
            V((d_in, hid), bf16),
            V((total, hid), bf16),
            V((hid, d_out), bf16),
            V((STEPS, total, d_out), bf16),
            V((STEPS, nb, rows, d_out), bf16),
            V((STEPS, total, d_out), bf16),
            D((15,)), D((nb,)), D((nb,)),
            D((STEPS, nb)), D((STEPS, nb)), D((STEPS, nb)), D((STEPS, nb)),
            D((7,)), D((7,)), D((nb,)), D((nb,)),
        ],
        compiler_params=pltpu.CompilerParams(
            collective_id=0, has_side_effects=True, vmem_limit_bytes=40 * 1024 * 1024
        ),
    )(x_in, t_in, row_picks, l1, l2, n1h, n2h)
    grad = lax.dot_general(xx, cc, TN, preferred_element_type=f32)
    moved_a = dd.astype(f32) - (half_step * scale_in) * grad
    return moved_a[None], m2.astype(f32)[None], errs[None]


def solution(mesh):
    in_specs = (
        P("shard", "batch", None),
        P("shard", "batch", None),
        P(None, "shard", "batch"),
        P("shard", None, "batch"),
        P("shard", "batch", None),
        P(None, "shard", None, "batch"),
        P(None, "shard", "batch", None),
    )
    out_specs = (P("shard", None, "batch"), P("shard", "batch", None), P("shard", "batch", None))
    return jax.shard_map(
        functools.partial(per_device, mesh.shape["shard"], mesh.shape["batch"]),
        mesh=mesh, in_specs=in_specs, out_specs=out_specs, check_vma=False,
    )
```

```python
import functools

import jax
import jax.numpy as jnp
from jax import lax
from jax.experimental import pallas as pl
from jax.experimental.pallas import tpu as pltpu
from jax.sharding import PartitionSpec as P

D_IN = 1024
HID = 2048
STEPS = 2
half_step = 0.01
keep = 1.0 - half_step
root_step = 0.02**0.5
precision_obs = 32.0
scale_in = D_IN ** (-0.5)
scale_hid = HID ** (-0.5)
MESH = pl.DeviceIdType.MESH
TN = (((0,), (0,)), ((), ()))
NT = (((1,), (1,)), ((), ()))
f32 = jnp.float32
bf16 = jnp.bfloat16


def kernel(
    ns, nb, x_in, t_in, picks, l1, l2, n1h, n2h,
    d_out, x_out, c_out, m2_out, errs,
    x, w1, w2, n1, n2, w1b, w2b, h, hb, bh0, dsend, csend, m2send, share, share_in, sw,
    load_sem, xs_sem, xr_sem, ss_sem, sr_sem, gs_sem, gr_sem, hs_sem, hr_sem, fs_sem, fr_sem,
):
    s = lax.axis_index("shard")
    b = lax.axis_index("batch")
    nxt = (lax.rem(s + 1, ns), b)
    prv = (lax.rem(s + ns - 1, ns), b)
    rows = x_in.shape[0]

    quarter = D_IN // 4
    pairs = []
    for q in range(4):
        piece = pl.ds(q * quarter, quarter)
        pairs += [(l1.at[piece], w1.at[piece])]
        pairs += [(n1h.at[i, piece], n1.at[i, piece]) for i in range(STEPS)]
    pairs += [(l2, w2)] + [(n2h.at[i], n2.at[i]) for i in range(STEPS)]
    loads = [
        pltpu.make_async_copy(src, dst, load_sem.at[i]) for i, (src, dst) in enumerate(pairs)
    ]
    for load in loads:
        load.start()

    barrier = pltpu.get_barrier_semaphore()
    peers = [(s, lax.rem(b + k, nb)) for k in range(nb)]
    owners = [(s, lax.rem(b + nb - k, nb)) for k in range(nb)]
    for who in peers[1:] + [nxt, prv]:
        pl.semaphore_signal(barrier, inc=1, device_id=who, device_id_type=MESH)
    pl.semaphore_wait(barrier, nb + 1)

    sends = []

    def remote(src, dst, send, recv, who):
        copy = pltpu.make_async_remote_copy(
            src_ref=src, dst_ref=dst, send_sem=send, recv_sem=recv,
            device_id=who, device_id_type=MESH,
        )
        copy.start()
        sends.append(copy)
        return copy

    def slot(k):
        return pl.ds(k * rows, rows)

    gathers = [
        remote(x_in, x.at[slot(k)], xs_sem.at[k], xr_sem.at[k], peers[k])
        for k in range(1, nb)
    ]
    passed = remote(x_in, x_out.at[slot(0)], hs_sem.at[4], hr_sem.at[4], nxt)
    x[slot(0), :] = x_in[...]

    hops = []
    for q in range(4):
        for load in loads[3 * q : 3 * q + 3]:
            load.wait()

        @pl.loop(0, quarter, step=32)
        def _(r, q=q):
            part = pl.ds(q * quarter + r, 32)
            w = w1[part, :]
            w1b[part, :] = w.astype(bf16)
            w = keep * w + root_step * n1[0, part, :].astype(f32)
            w1[part, :] = w
            dsend[part, :] = (keep * w + root_step * n1[1, part, :].astype(f32)).astype(bf16)
        piece = pl.ds(q * quarter, quarter)
        hops.append(remote(dsend.at[piece], d_out.at[piece], hs_sem.at[q], hr_sem.at[q], nxt))
    for load in loads[12:]:
        load.wait()
    for copy in gathers:
        copy.wait_recv()

    for step in range(STEPS):
        w2b[...] = w2[...].astype(bf16)
        hidden = jnp.tanh(jnp.dot(x[...], w1b[...], preferred_element_type=f32) * scale_in)
        h[...] = hidden
        hb[...] = hidden.astype(bf16)
        share[step] = (
            jnp.dot(hb[...], w2b[...], preferred_element_type=f32) * scale_hid
        ).astype(bf16)
        scatters = [
            remote(
                share.at[step, slot(k)], share_in.at[step, k],
                ss_sem.at[step, k], sr_sem.at[step, k], owners[k],
            )
            for k in range(1, nb)
        ]
        @pl.loop(0, w2.shape[0], step=32)
        def _(r):
            part = pl.ds(r, 32)
            w2[part, :] = keep * w2[part, :] + root_step * n2[step, part, :].astype(f32)

        picked = lax.broadcasted_iota(jnp.int32, (rows, picks.shape[2]), 0) == picks[step]
        picked = jnp.where(picked, 1.0, 0.0)
        counts = jnp.sum(picked, axis=1, keepdims=True)
        predicted = share[step, slot(0), :].astype(f32)
        for k in range(1, nb):
            scatters[k - 1].wait_recv()
            predicted = predicted + share_in[step, k].astype(f32)
        errors = predicted - t_in[...].astype(f32)
        signal = (precision_obs * errors).astype(bf16).astype(f32)
        sw[step, slot(0), :] = (counts * signal).astype(bf16)
        signals = [
            remote(
                sw.at[step, slot(0)], sw.at[step, slot(k)],
                gs_sem.at[step, k], gr_sem.at[step, k], peers[k],
            )
            for k in range(1, nb)
        ]
        if step == STEPS - 1:
            errs[...] = lax.dot_general(
                picked.astype(bf16), errors.astype(bf16), TN, preferred_element_type=f32
            ).astype(bf16)
        for copy in signals:
            copy.wait_recv()
        back = (
            lax.dot_general(sw[step], w2b[...], NT, preferred_element_type=f32)
            * scale_hid
            * (1.0 - h[...] * h[...])
        )
        if step == 0:
            bh0[...] = back.astype(bf16)
        else:
            csend[...] = (keep * bh0[...].astype(f32) + back).astype(bf16)
            hops.append(remote(csend, c_out, hs_sem.at[5], hr_sem.at[5], nxt))
        grad_two = lax.dot_general(hb[...], sw[step], TN, preferred_element_type=f32)
        final_two = w2[...] - (half_step * scale_hid) * grad_two
        if step == 0:
            w2[...] = final_two
            for q in range(4):
                piece = pl.ds(q * quarter, quarter)
                grad_one = lax.dot_general(x[:, piece], bh0[...], TN, preferred_element_type=f32)
                w1b[piece, :] = (w1[piece, :] - (half_step * scale_in) * grad_one).astype(bf16)
        else:
            m2send[...] = final_two.astype(bf16)
            hops.append(remote(m2send, m2_out, hs_sem.at[6], hr_sem.at[6], nxt))
    passed.wait_recv()
    hops += [
        remote(x_out.at[slot(0)], x_out.at[slot(k)], fs_sem.at[k], fr_sem.at[k], peers[k])
        for k in range(1, nb)
    ]

    for copy in hops:
        copy.wait_recv()
    for copy in sends:
        copy.wait_send()


def per_device(ns, nb, data_inputs, data_targets, row_picks, layer_one, layer_two, noise_one, noise_two):
    x_in, t_in, l1, l2 = data_inputs[0], data_targets[0], layer_one[0], layer_two[0]
    n1h, n2h = noise_one[:, 0], noise_two[:, 0]
    rows, d_in = x_in.shape
    d_out = t_in.shape[1]
    hid = l1.shape[1]
    total = rows * nb
    mine = row_picks.shape[2]
    any_spec = pl.BlockSpec(memory_space=pl.ANY)
    vmem = pl.BlockSpec(memory_space=pltpu.VMEM)
    V = pltpu.VMEM
    D = pltpu.SemaphoreType.DMA
    dd, xx, cc, m2, errs = pl.pallas_call(
        functools.partial(kernel, ns, nb),
        out_shape=(
            jax.ShapeDtypeStruct((d_in, hid), bf16),
            jax.ShapeDtypeStruct((total, d_in), bf16),
            jax.ShapeDtypeStruct((total, hid), bf16),
            jax.ShapeDtypeStruct((hid, d_out), bf16),
            jax.ShapeDtypeStruct((mine, d_out), bf16),
        ),
        in_specs=[vmem] * 3 + [any_spec] * 4,
        out_specs=(any_spec,) * 4 + (vmem,),
        scratch_shapes=[
            V((total, d_in), bf16),
            V((d_in, hid), f32),
            V((hid, d_out), f32),
            V((STEPS, d_in, hid), bf16),
            V((STEPS, hid, d_out), bf16),
            V((d_in, hid), bf16),
            V((hid, d_out), bf16),
            V((total, hid), f32),
            V((total, hid), bf16),
            V((total, hid), bf16),
            V((d_in, hid), bf16),
            V((total, hid), bf16),
            V((hid, d_out), bf16),
            V((STEPS, total, d_out), bf16),
            V((STEPS, nb, rows, d_out), bf16),
            V((STEPS, total, d_out), bf16),
            D((15,)), D((nb,)), D((nb,)),
            D((STEPS, nb)), D((STEPS, nb)), D((STEPS, nb)), D((STEPS, nb)),
            D((7,)), D((7,)), D((nb,)), D((nb,)),
        ],
        compiler_params=pltpu.CompilerParams(
            collective_id=0, has_side_effects=True, vmem_limit_bytes=60 * 1024 * 1024
        ),
    )(x_in, t_in, row_picks, l1, l2, n1h, n2h)
    grad = lax.dot_general(xx, cc, TN, preferred_element_type=f32)
    moved_a = dd.astype(f32) - (half_step * scale_in) * grad
    return moved_a[None], m2.astype(f32)[None], errs[None]


def solution(mesh):
    in_specs = (
        P("shard", "batch", None),
        P("shard", "batch", None),
        P(None, "shard", "batch"),
        P("shard", None, "batch"),
        P("shard", "batch", None),
        P(None, "shard", None, "batch"),
        P(None, "shard", "batch", None),
    )
    out_specs = (P("shard", None, "batch"), P("shard", "batch", None), P("shard", "batch", None))
    return jax.shard_map(
        functools.partial(per_device, mesh.shape["shard"], mesh.shape["batch"]),
        mesh=mesh, in_specs=in_specs, out_specs=out_specs, check_vma=False,
    )
```

```python
import functools

import jax
import jax.numpy as jnp
from jax import lax
from jax.experimental import pallas as pl
from jax.experimental.pallas import tpu as pltpu
from jax.sharding import PartitionSpec as P

D_IN = 1024
HID = 2048
STEPS = 2
half_step = 0.01
keep = 1.0 - half_step
root_step = 0.02**0.5
precision_obs = 32.0
scale_in = D_IN ** (-0.5)
scale_hid = HID ** (-0.5)
MESH = pl.DeviceIdType.MESH
TN = (((0,), (0,)), ((), ()))
NT = (((1,), (1,)), ((), ()))
f32 = jnp.float32
bf16 = jnp.bfloat16


def kernel(
    ns, nb, x_in, t_in, picks, l1, l2, n1h, n2h,
    d_out, x_out, c_out, m2_out, errs,
    x, w1, w2, n1, n2, w1b, w2b, h, hb, bh0, dsend, csend, m2send, share, share_in, sw,
    load_sem, xs_sem, xr_sem, ss_sem, sr_sem, gs_sem, gr_sem, hs_sem, hr_sem, fs_sem, fr_sem,
):
    s = lax.axis_index("shard")
    b = lax.axis_index("batch")
    nxt = (lax.rem(s + 1, ns), b)
    prv = (lax.rem(s + ns - 1, ns), b)
    rows = x_in.shape[0]

    quarter = D_IN // 4
    pairs = []
    for q in range(4):
        piece = pl.ds(q * quarter, quarter)
        pairs += [(l1.at[piece], w1.at[piece])]
        pairs += [(n1h.at[i, piece], n1.at[i, piece]) for i in range(STEPS)]
    pairs += [(l2, w2)] + [(n2h.at[i], n2.at[i]) for i in range(STEPS)]
    order = [0, 3, 6, 9, 12, 1, 2, 4, 5, 7, 8, 10, 11, 13, 14]
    pairs = [pairs[i] for i in order]
    loads = [
        pltpu.make_async_copy(src, dst, load_sem.at[i]) for i, (src, dst) in enumerate(pairs)
    ]
    for load in loads:
        load.start()

    barrier = pltpu.get_barrier_semaphore()
    peers = [(s, lax.rem(b + k, nb)) for k in range(nb)]
    owners = [(s, lax.rem(b + nb - k, nb)) for k in range(nb)]
    for who in peers[1:] + [nxt, prv]:
        pl.semaphore_signal(barrier, inc=1, device_id=who, device_id_type=MESH)
    pl.semaphore_wait(barrier, nb + 1)

    sends = []

    def remote(src, dst, send, recv, who):
        copy = pltpu.make_async_remote_copy(
            src_ref=src, dst_ref=dst, send_sem=send, recv_sem=recv,
            device_id=who, device_id_type=MESH,
        )
        copy.start()
        sends.append(copy)
        return copy

    def slot(k):
        return pl.ds(k * rows, rows)

    gathers = [
        remote(x_in, x.at[slot(k)], xs_sem.at[k], xr_sem.at[k], peers[k])
        for k in range(1, nb)
    ]
    passed = remote(x_in, x_out.at[slot(0)], hs_sem.at[4], hr_sem.at[4], nxt)
    x[slot(0), :] = x_in[...]

    hops = []
    for q in range(4):
        loads[q].wait()

        @pl.loop(0, quarter, step=32)
        def _(r, q=q):
            part = pl.ds(q * quarter + r, 32)
            w1b[part, :] = w1[part, :].astype(bf16)
    loads[4].wait()
    for copy in gathers:
        copy.wait_recv()

    for step in range(STEPS):
        w2b[...] = w2[...].astype(bf16)
        hidden = jnp.tanh(jnp.dot(x[...], w1b[...], preferred_element_type=f32) * scale_in)
        h[...] = hidden
        hb[...] = hidden.astype(bf16)
        share[step] = (
            jnp.dot(hb[...], w2b[...], preferred_element_type=f32) * scale_hid
        ).astype(bf16)
        scatters = [
            remote(
                share.at[step, slot(k)], share_in.at[step, k],
                ss_sem.at[step, k], sr_sem.at[step, k], owners[k],
            )
            for k in range(1, nb)
        ]
        if step == 0:
            for q in range(4):
                for load in loads[5 + 2 * q : 7 + 2 * q]:
                    load.wait()

                @pl.loop(0, quarter, step=32)
                def _(r, q=q):
                    part = pl.ds(q * quarter + r, 32)
                    w = w1[part, :]
                    w = keep * w + root_step * n1[0, part, :].astype(f32)
                    w1[part, :] = w
                    dsend[part, :] = (keep * w + root_step * n1[1, part, :].astype(f32)).astype(bf16)
                piece = pl.ds(q * quarter, quarter)
                hops.append(remote(dsend.at[piece], d_out.at[piece], hs_sem.at[q], hr_sem.at[q], nxt))
            for load in loads[13:]:
                load.wait()

        @pl.loop(0, w2.shape[0], step=32)
        def _(r):
            part = pl.ds(r, 32)
            w2[part, :] = keep * w2[part, :] + root_step * n2[step, part, :].astype(f32)

        picked = lax.broadcasted_iota(jnp.int32, (rows, picks.shape[2]), 0) == picks[step]
        picked = jnp.where(picked, 1.0, 0.0)
        counts = jnp.sum(picked, axis=1, keepdims=True)
        predicted = share[step, slot(0), :].astype(f32)
        for k in range(1, nb):
            scatters[k - 1].wait_recv()
            predicted = predicted + share_in[step, k].astype(f32)
        errors = predicted - t_in[...].astype(f32)
        signal = (precision_obs * errors).astype(bf16).astype(f32)
        sw[step, slot(0), :] = (counts * signal).astype(bf16)
        signals = [
            remote(
                sw.at[step, slot(0)], sw.at[step, slot(k)],
                gs_sem.at[step, k], gr_sem.at[step, k], peers[k],
            )
            for k in range(1, nb)
        ]
        if step == STEPS - 1:
            errs[...] = lax.dot_general(
                picked.astype(bf16), errors.astype(bf16), TN, preferred_element_type=f32
            ).astype(bf16)
        for copy in signals:
            copy.wait_recv()
        back = (
            lax.dot_general(sw[step], w2b[...], NT, preferred_element_type=f32)
            * scale_hid
            * (1.0 - h[...] * h[...])
        )
        if step == 0:
            bh0[...] = back.astype(bf16)
        else:
            csend[...] = (keep * bh0[...].astype(f32) + back).astype(bf16)
            hops.append(remote(csend, c_out, hs_sem.at[5], hr_sem.at[5], nxt))
        grad_two = lax.dot_general(hb[...], sw[step], TN, preferred_element_type=f32)
        final_two = w2[...] - (half_step * scale_hid) * grad_two
        if step == 0:
            w2[...] = final_two
            for q in range(4):
                piece = pl.ds(q * quarter, quarter)
                grad_one = lax.dot_general(x[:, piece], bh0[...], TN, preferred_element_type=f32)
                w1b[piece, :] = (w1[piece, :] - (half_step * scale_in) * grad_one).astype(bf16)
        else:
            m2send[...] = final_two.astype(bf16)
            hops.append(remote(m2send, m2_out, hs_sem.at[6], hr_sem.at[6], nxt))
    passed.wait_recv()
    hops += [
        remote(x_out.at[slot(0)], x_out.at[slot(k)], fs_sem.at[k], fr_sem.at[k], peers[k])
        for k in range(1, nb)
    ]

    for copy in hops:
        copy.wait_recv()
    for copy in sends:
        copy.wait_send()


def per_device(ns, nb, data_inputs, data_targets, row_picks, layer_one, layer_two, noise_one, noise_two):
    x_in, t_in, l1, l2 = data_inputs[0], data_targets[0], layer_one[0], layer_two[0]
    n1h, n2h = noise_one[:, 0], noise_two[:, 0]
    rows, d_in = x_in.shape
    d_out = t_in.shape[1]
    hid = l1.shape[1]
    total = rows * nb
    mine = row_picks.shape[2]
    any_spec = pl.BlockSpec(memory_space=pl.ANY)
    vmem = pl.BlockSpec(memory_space=pltpu.VMEM)
    V = pltpu.VMEM
    D = pltpu.SemaphoreType.DMA
    dd, xx, cc, m2, errs = pl.pallas_call(
        functools.partial(kernel, ns, nb),
        out_shape=(
            jax.ShapeDtypeStruct((d_in, hid), bf16),
            jax.ShapeDtypeStruct((total, d_in), bf16),
            jax.ShapeDtypeStruct((total, hid), bf16),
            jax.ShapeDtypeStruct((hid, d_out), bf16),
            jax.ShapeDtypeStruct((mine, d_out), bf16),
        ),
        in_specs=[vmem] * 3 + [any_spec] * 4,
        out_specs=(any_spec,) * 4 + (vmem,),
        scratch_shapes=[
            V((total, d_in), bf16),
            V((d_in, hid), f32),
            V((hid, d_out), f32),
            V((STEPS, d_in, hid), bf16),
            V((STEPS, hid, d_out), bf16),
            V((d_in, hid), bf16),
            V((hid, d_out), bf16),
            V((total, hid), f32),
            V((total, hid), bf16),
            V((total, hid), bf16),
            V((d_in, hid), bf16),
            V((total, hid), bf16),
            V((hid, d_out), bf16),
            V((STEPS, total, d_out), bf16),
            V((STEPS, nb, rows, d_out), bf16),
            V((STEPS, total, d_out), bf16),
            D((15,)), D((nb,)), D((nb,)),
            D((STEPS, nb)), D((STEPS, nb)), D((STEPS, nb)), D((STEPS, nb)),
            D((7,)), D((7,)), D((nb,)), D((nb,)),
        ],
        compiler_params=pltpu.CompilerParams(
            collective_id=0, has_side_effects=True, vmem_limit_bytes=60 * 1024 * 1024
        ),
    )(x_in, t_in, row_picks, l1, l2, n1h, n2h)
    grad = lax.dot_general(xx, cc, TN, preferred_element_type=f32)
    moved_a = dd.astype(f32) - (half_step * scale_in) * grad
    return moved_a[None], m2.astype(f32)[None], errs[None]


def solution(mesh):
    in_specs = (
        P("shard", "batch", None),
        P("shard", "batch", None),
        P(None, "shard", "batch"),
        P("shard", None, "batch"),
        P("shard", "batch", None),
        P(None, "shard", None, "batch"),
        P(None, "shard", "batch", None),
    )
    out_specs = (P("shard", None, "batch"), P("shard", "batch", None), P("shard", "batch", None))
    return jax.shard_map(
        functools.partial(per_device, mesh.shape["shard"], mesh.shape["batch"]),
        mesh=mesh, in_specs=in_specs, out_specs=out_specs, check_vma=False,
    )
```
